256 devices in a mesh: own: 16 (over z, core), pair: 16 (over y, x).
Axes of the slice: x: 4, y: 4, z: 8, core: 2. Of those that a mesh axis runs over, the one named last changes fastest.
Arguments:
- residual: bfloat16 [262144, 512], P(('own', 'pair')), may hold values from -8 to 8
- code_one: int32 [262144], P(('own', 'pair')), may hold values from 0 to 8191, as said below
- code_two: int32 [262144], P(('own', 'pair')), may hold values from 0 to 8191, as said below
Outputs:
- final_residual: bfloat16 [262144, 512], P(('own', 'pair'))
- nearness: bfloat16 [262144, 512], P(('own', 'pair'))
The draws below stay inside these ranges and needn't reach their ends.
Inputs may be any that keep to these rules, and one draw needn't show every extreme that they name: `code_one`: the owner group of a code is code // 512. Of the 1024 items of one device (devices counted in mesh order, own first), the number whose code lies in owner group o depends only on (o + device) mod 16, is at most 128, and equals 128 for some group on every device. Every code is held by exactly 32 items. `code_two`: same law as code_one, drawn independently.
All inputs are finite; a program needn't handle non-finite values.
Results may differ from the reference program's by a relative error of at most 0.012.
Values may be sent and summed in bfloat16 or wider, within the bound.
A program may use at most 64 MiB of HBM per device.

```python
import jax
import jax.numpy as jnp
from jax import lax

D = 512
K = 8192
ROWS_DEV = 1024
ROWS = 262144
N_OWN = 16
N_PAIR = 16


def owner_codes(key):
    rank_key, shuffle_key, visit_key = jax.random.split(key, 3)
    mean_load = ROWS_DEV // N_OWN
    rank_ids = jnp.arange(N_OWN, dtype=jnp.int32)
    load_table = jnp.where(rank_ids % 2 == 0, 3 * mean_load // 2, mean_load // 2)
    load_table = jnp.where(rank_ids == 0, 2 * mean_load, jnp.where(rank_ids == 1, 0, load_table))
    rank_perm = jax.random.permutation(rank_key, N_OWN)
    blocks = N_OWN * N_PAIR
    block_ids = jnp.arange(blocks, dtype=jnp.int32)
    owners = jnp.arange(N_OWN, dtype=jnp.int32)
    rank_of = rank_perm[(owners[None, :] + block_ids[:, None]) % N_OWN]
    counts = load_table[rank_of]
    bounds = jnp.cumsum(counts, axis=1)
    slot_ids = jnp.arange(ROWS_DEV, dtype=jnp.int32)
    owner_list = jnp.sum((slot_ids[None, :, None] >= bounds[:, None, :]).astype(jnp.int32), axis=2)
    shuffle_keys = jax.random.split(shuffle_key, blocks)
    shuffles = jax.vmap(lambda sub_key: jax.random.permutation(sub_key, ROWS_DEV))(shuffle_keys)
    owner_rows = jnp.take_along_axis(owner_list, shuffles, axis=1).reshape(-1)
    visit_order = jax.random.permutation(visit_key, ROWS_DEV * blocks)
    visited = owner_rows[visit_order]
    matches = (visited[:, None] == owners[None, :]).astype(jnp.int32)
    rank_seen = jnp.sum(jnp.cumsum(matches, axis=0) * matches, axis=1) - 1
    owner_rank = jnp.zeros((ROWS_DEV * blocks,), jnp.int32).at[visit_order].set(rank_seen.astype(jnp.int32))
    per_owner = K // N_OWN
    return (owner_rows * per_owner + owner_rank % per_owner).astype(jnp.int32)


def clipped_normal(key, shape):
    return jnp.clip(jax.random.normal(key, shape, jnp.float32), -3.0, 3.0)


def draw_residual(key, part):
    first_codes = owner_codes(jax.random.fold_in(key, 11))
    second_codes = owner_codes(jax.random.fold_in(key, 23))
    key = jax.random.fold_in(key, 31)
    table_key, other_key, common_key, noise_key = jax.random.split(key, 4)
    group_of = jnp.arange(K, dtype=jnp.int32) // (K // N_OWN)
    table_one = 0.8 * clipped_normal(table_key, (K, D))
    common = clipped_normal(common_key, (N_OWN, D))
    table_two = 0.5 * common[group_of] + 0.7 * clipped_normal(other_key, (K, D))
    noise = 0.5 * clipped_normal(noise_key, (ROWS, D))
    return (table_one[first_codes] + table_two[second_codes] + noise).astype(jnp.bfloat16)


def draw_code_one(key, part):
    key = jax.random.fold_in(key, 11)
    return owner_codes(key)


def draw_code_two(key, part):
    key = jax.random.fold_in(key, 23)
    return owner_codes(key)


def setup_inputs(seed: int = 0) -> dict:
    key_list = jax.random.split(jax.random.key(seed), 4)
    residual = draw_residual(jax.random.fold_in(key_list[3], 71), 0)
    code_one = draw_code_one(jax.random.fold_in(key_list[3], 71), 0)
    code_two = draw_code_two(jax.random.fold_in(key_list[3], 71), 0)
    return {"residual": residual, "code_one": code_one, "code_two": code_two}


def centroids(row_block, codes):
    code_sums = jax.ops.segment_sum(row_block.astype(jnp.float32), codes, num_segments=K)
    counts = jax.ops.segment_sum(jnp.ones(codes.shape, jnp.float32), codes, num_segments=K)
    return (code_sums / counts[:, None]).astype(jnp.bfloat16)


def reference(residual, code_one, code_two):
    centroid_one = centroids(residual, code_one)
    second = (residual.astype(jnp.float32) - centroid_one[code_one].astype(jnp.float32)).astype(jnp.bfloat16)
    centroid_two = centroids(second, code_two)
    final_residual = (second.astype(jnp.float32) - centroid_two[code_two].astype(jnp.float32)).astype(jnp.bfloat16)
    per_owner = K // N_OWN
    owner_ids = (code_two // per_owner).astype(jnp.int32)
    sort_order = jnp.argsort(owner_ids, stable=True).astype(jnp.int32)
    grouped = second[sort_order].astype(jnp.float32).reshape(N_OWN, -1, D)
    centroid_blocks = centroid_two.astype(jnp.float32).reshape(N_OWN, per_owner, D)
    products = jnp.einsum("grd,gkd->grk", grouped, centroid_blocks, precision=lax.Precision.HIGHEST)
    squares = jnp.sum(grouped * grouped, axis=2)
    center_sq = jnp.sum(centroid_blocks * centroid_blocks, axis=2)
    near_grouped = (squares[:, :, None] - 2.0 * products + center_sq[:, None, :]) / D
    nearness = jnp.zeros((ROWS, per_owner), jnp.float32).at[sort_order].set(near_grouped.reshape(-1, per_owner))
    return final_residual, nearness.astype(jnp.bfloat16)
```

```python
import functools

import jax
import jax.numpy as jnp
from jax import lax
from jax.experimental import pallas as pl
from jax.experimental.pallas import tpu as pltpu
from jax.sharding import PartitionSpec as P

ROWS = 1024
D = 512
GROUPS = 16
CAP = 128
SLOTS = GROUPS * CAP
GCODES = 512
ITEMS_PER_CODE = 32
CHUNKS = 2
W = D // CHUNKS
HALF = GCODES // 2
ZN = 8
ZC = HALF // ZN
BF = jnp.bfloat16
F32 = jnp.float32
I32 = jnp.int32
NT = (((1,), (1,)), ((), ()))


def iota(shape, dim):
    return lax.broadcasted_iota(I32, shape, dim)


def hot(mask):
    return jnp.where(mask, 1.0, 0.0).astype(BF)


def prep_kernel(lane_ref, col_ref, rows_ref, packed_ref, send_ref, scol_ref, item_ref, tgt_ref):
    codes = lane_ref[...]
    groups = lax.shift_right_logical(codes, 9)
    member = jnp.concatenate(
        [
            iota((GROUPS, ROWS), 0) == groups[0:1, :],
            iota((GROUPS, ROWS), 0) == groups[1:2, :],
        ],
        axis=0,
    )
    before = hot(iota((ROWS, ROWS), 0) < iota((ROWS, ROWS), 1))
    rank = jnp.dot(hot(member), before, preferred_element_type=F32)
    rank = jnp.where(member, rank, 0.0)
    target = []
    for level in range(2):
        r = jnp.sum(rank[level * GROUPS : (level + 1) * GROUPS], axis=0, keepdims=True)
        target.append(groups[level : level + 1] * CAP + r.astype(I32))
    gcol = lax.shift_right_logical(col_ref[...], 9)[:, 1:2]
    mcol = iota((ROWS, 128), 1) == gcol
    after = hot(iota((ROWS, ROWS), 0) > iota((ROWS, ROWS), 1))
    rcol = jnp.dot(after, hot(mcol), preferred_element_type=F32)
    rcol = jnp.sum(jnp.where(mcol, rcol, 0.0), axis=1, keepdims=True)
    tgt_ref[...] = gcol * CAP + rcol.astype(I32)

    item = iota((1, ROWS), 1)
    send_ref[...] = jnp.zeros_like(send_ref)
    for level in range(2):
        local = jnp.bitwise_and(codes[level : level + 1], GCODES - 1)
        feats = jnp.concatenate(
            [
                lax.shift_right_logical(local, 4),
                jnp.bitwise_and(local, 15),
                lax.shift_right_logical(item, 5),
                jnp.bitwise_and(item, 31),
                jnp.ones_like(item),
                jnp.zeros((3, ROWS), I32),
            ],
            axis=0,
        ).astype(F32).astype(BF)

        def block(o, carry, level=level, feats=feats):
            base = pl.multiple_of(o * CAP, CAP)
            place = hot(iota((CAP, ROWS), 0) + base == target[level])
            if level == 0:
                got = jnp.dot(place, rows_ref[...], preferred_element_type=F32).astype(BF)
                for ch in range(CHUNKS):
                    packed_ref[ch, o] = got[:, ch * W : (ch + 1) * W]
            lanes = lax.dot_general(feats, place, NT, preferred_element_type=F32)
            live = lanes[4:5]
            send_ref[o, level : level + 1, :] = (lanes[0:1] * 16.0 + lanes[1:2] + live - 1.0).astype(I32)
            if level == 0:
                item_ref[o] = jnp.broadcast_to(lanes[2:3] * 32.0 + lanes[3:4] + live - 1.0, (8, CAP)).astype(I32)
            cols = lax.dot_general(place, feats, NT, preferred_element_type=F32)
            alive = cols[:, 4:5]
            code = (cols[:, 0:1] * 16.0 + cols[:, 1:2] + alive - 1.0).astype(I32)
            scol_ref[level, o, :, 0:1] = code
            which = (cols[:, 2:3] * 32.0 + cols[:, 3:4] + 2.0 * alive - 2.0).astype(I32)
            scol_ref[level, o, :, 1:2] = which
            return carry

        lax.fori_loop(0, GROUPS, block, 0)


def main_kernel(
    packed1, send_codes, scol, item1, tgt2,
    final_out, near_out,
    got_codes, packed2, got, acc, half_out, half_in, zpart, zin, table, move, back, secp, finp, nearacc, nearp,
    code_s, code_r, a2a_s, a2a_r, hs, hr, rzs, rzr, azs, azr, xs, xr, ss, sr,
):
    own = lax.axis_index("own")
    me = lax.axis_index("pair")
    z, c = lax.div(own, 2), lax.rem(own, 2)
    y, x = lax.div(me, 4), lax.rem(me, 4)
    sib = z * 2 + (1 - c)

    def at(dy, dx):
        return lax.rem(y + dy, 4) * 4 + lax.rem(x + dx, 4)

    def zat(dz):
        return lax.rem(z + dz, ZN) * 2 + c

    barrier = pltpu.get_barrier_semaphore()

    def greet(o, p):
        pl.semaphore_signal(barrier, inc=1, device_id=(o, p), device_id_type=pl.DeviceIdType.MESH)

    for d in range(1, 16):
        greet(own, at(d // 4, d % 4))
    for dz in range(1, ZN):
        greet(zat(dz), me)
    greet(sib, me)
    pl.semaphore_wait(barrier, 15 + ZN - 1 + 1)

    started = []

    def copy(src, dst, s, r, o, p):
        return pltpu.make_async_remote_copy(
            src_ref=src, dst_ref=dst, send_sem=s, recv_sem=r,
            device_id=(o, p), device_id_type=pl.DeviceIdType.MESH,
        )

    def send(src, dst, s, r, o, p):
        k = copy(src, dst, s, r, o, p)
        k.start()
        started.append(k)

    def arrive(dst, s, r):
        copy(dst, dst, s, r, own, at(0, 1)).wait_recv()

    packs = (packed1, packed2)
    order = [(0, 1), (1, 0), (0, 3), (3, 0), (1, 1), (3, 3), (1, 3), (3, 1),
             (0, 2), (2, 0), (1, 2), (2, 1), (3, 2), (2, 3), (2, 2)]

    def send_rows(l, ch, dy, dx):
        d = dy * 4 + dx
        to = at(dy, dx)
        send(packs[l].at[ch, to], got.at[l, ch, d], a2a_s.at[l, ch, d], a2a_r.at[l, ch, d], own, to)

    def sum_rows(l, ch):
        got[l, ch, 0] = packs[l][ch, me]
        for q in range(4):
            for d in range(4 * q, 4 * q + 4):
                if d:
                    arrive(got.at[l, ch, d], a2a_s.at[l, ch, d], a2a_r.at[l, ch, d])
                    if l == 0 and ch == 0:
                        arrive(got_codes.at[d], code_s.at[d], code_r.at[d])
            codes = jnp.concatenate([got_codes[d, l : l + 1, :] for d in range(4 * q, 4 * q + 4)], axis=1)
            pick = hot(iota((GCODES, 4 * CAP), 0) == codes)
            part = jnp.dot(pick, got[l, ch, 4 * q : 4 * q + 4].reshape(4 * CAP, W), preferred_element_type=F32)
            if q == 0:
                acc[ch] = part
            else:
                acc[ch] += part
        half_out[l, ch] = acc[ch, pl.ds(pl.multiple_of((1 - c) * HALF, HALF), HALF)].astype(BF)
        send(half_out.at[l, ch], half_in.at[l, ch], hs.at[l, ch], hr.at[l, ch], sib, me)

    def reduce_z(l, ch):
        arrive(half_in.at[l, ch], hs.at[l, ch], hr.at[l, ch])
        mine = pl.ds(pl.multiple_of(c * HALF, HALF), HALF)
        both = acc[ch, mine] + half_in[l, ch].astype(F32)
        acc[ch, mine] = both
        zpart[l, ch] = both.astype(BF)
        for dz in (1, 7, 2, 6, 3, 5, 4):
            to = lax.rem(z + dz, ZN)
            send(zpart.at[l, ch, pl.ds(pl.multiple_of(to * ZC, ZC), ZC)], zin.at[l, ch, dz],
                 rzs.at[l, ch, dz], rzr.at[l, ch, dz], zat(dz), me)

    def gather_z(l, ch):
        total = acc[ch, pl.ds(pl.multiple_of(c * HALF + z * ZC, ZC), ZC)]
        for dz in range(1, ZN):
            arrive(zin.at[l, ch, dz], rzs.at[l, ch, dz], rzr.at[l, ch, dz])
            total += zin[l, ch, dz].astype(F32)
        mine = pl.ds(pl.multiple_of(z * ZC, ZC), ZC)
        table[l, ch, 0, c, mine, :] = (total * (1.0 / ITEMS_PER_CODE)).astype(BF)
        for dz in (1, 7, 2, 6, 3, 5, 4):
            here = table.at[l, ch, 0, c, mine]
            send(here, here, azs.at[l, ch, dz], azr.at[l, ch, dz], zat(dz), me)

    def slot(ch, da, db):
        return da * 4 + db if ch % 2 == 0 else db * 4 + da

    def side(ch, da, db):
        return at(da, db) if ch % 2 == 0 else at(db, da)

    def to_sibling(l, ch, s):
        here = table.at[l, ch, s, c]
        send(here, here, ss.at[l, ch, s], sr.at[l, ch, s], sib, me)

    def pass_on(l, ch, source, dest, k, da, db, part):
        if part is None:
            a, b = table.at[l, ch, source, c], table.at[l, ch, dest, c]
        else:
            rows = pl.ds(part * (HALF // 2), HALF // 2)
            a, b = table.at[l, ch, source, c, rows], table.at[l, ch, dest, c, rows]
        send(a, b, xs.at[l, ch, k], xr.at[l, ch, k], own, side(ch, da, db))

    def come(l, ch, dest, k, part=None):
        if part is None:
            b = table.at[l, ch, dest, c]
        else:
            b = table.at[l, ch, dest, c, pl.ds(part * (HALF // 2), HALF // 2)]
        arrive(b, xs.at[l, ch, k], xr.at[l, ch, k])

    def second_axis(l, ch, da):
        s = slot(ch, da, 0)
        pass_on(l, ch, s, slot(ch, da, 1), 4 + 4 * da, 0, 1, None)
        pass_on(l, ch, s, slot(ch, da, 3), 5 + 4 * da, 0, 3, None)

    def start_plane(l, ch):
        here = table.at[l, ch, 0, c, pl.ds(0, ZC)]
        for dz in range(1, ZN):
            arrive(here, azs.at[l, ch, dz], azr.at[l, ch, dz])
        pass_on(l, ch, 0, slot(ch, 1, 0), 0, 1, 0, None)
        pass_on(l, ch, 0, slot(ch, 3, 0), 1, 3, 0, None)
        second_axis(l, ch, 0)
        to_sibling(l, ch, 0)

    def first_hop(l, ch, da):
        s, k = slot(ch, da, 0), (0 if da == 1 else 1)
        come(l, ch, s, k)
        if da == 1:
            pass_on(l, ch, s, slot(ch, 2, 0), 2, 1, 0, 0)
        else:
            pass_on(l, ch, s, slot(ch, 2, 0), 3, 3, 0, 1)
        second_axis(l, ch, da)
        to_sibling(l, ch, s)

    def first_far(l, ch):
        s = slot(ch, 2, 0)
        come(l, ch, s, 2, 0)
        come(l, ch, s, 3, 1)
        second_axis(l, ch, 2)
        to_sibling(l, ch, s)

    def second_hop(l, ch, da):
        s = slot(ch, da, 1)
        come(l, ch, s, 4 + 4 * da)
        pass_on(l, ch, s, slot(ch, da, 2), 6 + 4 * da, 0, 1, 0)
        to_sibling(l, ch, s)
        s = slot(ch, da, 3)
        come(l, ch, s, 5 + 4 * da)
        pass_on(l, ch, s, slot(ch, da, 2), 7 + 4 * da, 0, 3, 1)
        to_sibling(l, ch, s)

    def second_far(l, ch, da):
        s = slot(ch, da, 2)
        come(l, ch, s, 6 + 4 * da, 0)
        come(l, ch, s, 7 + 4 * da, 1)
        to_sibling(l, ch, s)

    def plane(l, ch, use):
        first_hop(l, ch, 1)
        first_hop(l, ch, 3)
        second_hop(l, ch, 0)
        use(slot(ch, 0, 0))
        first_far(l, ch)
        second_hop(l, ch, 1)
        second_hop(l, ch, 3)
        use(slot(ch, 1, 0))
        use(slot(ch, 3, 0))
        use(slot(ch, 0, 1))
        use(slot(ch, 0, 3))
        second_hop(l, ch, 2)
        second_far(l, ch, 0)
        second_far(l, ch, 1)
        second_far(l, ch, 3)
        use(slot(ch, 2, 0))
        for da in (1, 3):
            use(slot(ch, da, 1))
            use(slot(ch, da, 3))
        second_far(l, ch, 2)
        for da, db in ((0, 2), (2, 1), (2, 3), (1, 2), (3, 2), (2, 2)):
            use(slot(ch, da, db))

    def ready(l, ch, s):
        arrive(table.at[l, ch, s, 1 - c], ss.at[l, ch, s], sr.at[l, ch, s])
        o = at((4 - s // 4) % 4, (4 - s % 4) % 4)
        pick = hot(iota((CAP, GCODES), 1) == scol[l, o, :, 0:1])
        cents = table[l, ch, s].reshape(GCODES, W)
        return o, cents, jnp.dot(pick, cents, preferred_element_type=F32)

    def use_one(ch, s):
        o, _, picked = ready(0, ch, s)
        rows = (packed1[ch, o].astype(F32) - picked).astype(BF)
        secp[ch, pl.ds(pl.multiple_of(o * CAP, CAP), CAP), :] = rows

    def use_two(ch, s):
        o, cents, picked = ready(1, ch, s)
        place = pl.ds(pl.multiple_of(o * CAP, CAP), CAP)
        rows = packed2[ch, o]
        wide = rows.astype(F32)
        finp[ch, place, :] = (wide - picked).astype(BF)
        prods = lax.dot_general(rows, cents, NT, preferred_element_type=F32)
        sq = jnp.sum(wide * wide, axis=1, keepdims=True)
        cw = cents.astype(F32)
        cw = cw * cw
        top = cw.astype(BF)
        low = (cw - top.astype(F32)).astype(BF)
        ones = jnp.ones((8, W), BF)
        csq = lax.dot_general(ones, top, NT, preferred_element_type=F32)
        csq += lax.dot_general(ones, low, NT, preferred_element_type=F32)
        part = sq - 2.0 * prods + csq[0:1]
        if ch == 0:
            nearacc[place, :] = part
        elif ch < CHUNKS - 1:
            nearacc[place, :] += part
        else:
            nearp[place, :] = ((nearacc[place, :] + part) * (1.0 / D)).astype(BF)

    for dy, dx in order:
        d = dy * 4 + dx
        send(send_codes.at[at(dy, dx)], got_codes.at[d], code_s.at[d], code_r.at[d], own, at(dy, dx))
    got_codes[0] = send_codes[me]
    for ch in range(CHUNKS):
        for dy, dx in order:
            send_rows(0, ch, dy, dx)

    first_items = jnp.concatenate([item1[o, 0:1, :] for o in range(GROUPS)], axis=1)

    def build_move(o, carry):
        move[pl.ds(pl.multiple_of(o * CAP, CAP), CAP), :] = hot(first_items == scol[1, o, :, 1:2])
        return carry

    lax.fori_loop(0, GROUPS, build_move, 0)

    def build_back(b, carry):
        rows = pl.ds(pl.multiple_of(b * CAP, CAP), CAP)
        back[rows, :] = hot(iota((CAP, SLOTS), 1) == tgt2[rows, :])
        return carry

    lax.fori_loop(0, ROWS // CAP, build_back, 0)

    for l in range(2):
        for ch in range(CHUNKS):
            sum_rows(l, ch)
            reduce_z(l, ch)
            gather_z(l, ch)
            start_plane(l, ch)
        for ch in range(CHUNKS):
            if l == 0:
                plane(l, ch, functools.partial(use_one, ch))
                for dy in range(4):
                    oy = lax.rem(y + dy, 4)
                    rows = move[pl.ds(pl.multiple_of(oy * (4 * CAP), 4 * CAP), 4 * CAP), :]
                    moved = jnp.dot(rows, secp[ch], preferred_element_type=F32).astype(BF)
                    packed2[ch, pl.ds(oy * 4, 4)] = moved.reshape(4, CAP, W)
                    for dx in (1, 3, 0, 2):
                        if dy or dx:
                            send_rows(1, ch, dy, dx)
            else:
                plane(l, ch, functools.partial(use_two, ch))
                for b in range(2):
                    rows = back[b * 512 : (b + 1) * 512, :]
                    out = jnp.dot(rows, finp[ch], preferred_element_type=F32).astype(BF)
                    final_out[b * 512 : (b + 1) * 512, ch * W : (ch + 1) * W] = out
    for b in range(2):
        rows = back[b * 512 : (b + 1) * 512, :]
        near_out[b * 512 : (b + 1) * 512, :] = jnp.dot(rows, nearp[...], preferred_element_type=F32).astype(BF)
    for k in started:
        k.wait_send()


def vmem(n):
    return [pl.BlockSpec(memory_space=pltpu.VMEM)] * n


def per_device(residual, code_one, code_two):
    lanes = jnp.stack([code_one, code_two], axis=0)
    cols = jnp.stack([code_one, code_two], axis=1)
    packed, codes, scol, item, tgt = pl.pallas_call(
        prep_kernel,
        out_shape=(
            jax.ShapeDtypeStruct((CHUNKS, GROUPS, CAP, W), BF),
            jax.ShapeDtypeStruct((GROUPS, 8, CAP), I32),
            jax.ShapeDtypeStruct((2, GROUPS, CAP, 2), I32),
            jax.ShapeDtypeStruct((GROUPS, 8, CAP), I32),
            jax.ShapeDtypeStruct((ROWS, 1), I32),
        ),
        in_specs=vmem(3),
        out_specs=tuple(vmem(5)),
        compiler_params=pltpu.CompilerParams(vmem_limit_bytes=50 * 1024 * 1024),
    )(lanes, cols, residual)
    dma = pltpu.SemaphoreType.DMA
    C = CHUNKS
    out = pl.pallas_call(
        main_kernel,
        out_shape=(
            jax.ShapeDtypeStruct((ROWS, D), BF),
            jax.ShapeDtypeStruct((ROWS, D), BF),
        ),
        in_specs=vmem(5),
        out_specs=tuple(vmem(2)),
        scratch_shapes=[
            pltpu.VMEM((GROUPS, 8, CAP), I32),
            pltpu.VMEM((C, GROUPS, CAP, W), BF),
            pltpu.VMEM((2, C, GROUPS, CAP, W), BF),
            pltpu.VMEM((C, GCODES, W), F32),
            pltpu.VMEM((2, C, HALF, W), BF),
            pltpu.VMEM((2, C, HALF, W), BF),
            pltpu.VMEM((2, C, HALF, W), BF),
            pltpu.VMEM((2, C, ZN, ZC, W), BF),
            pltpu.VMEM((2, C, GROUPS, 2, HALF, W), BF),
            pltpu.VMEM((SLOTS, SLOTS), BF),
            pltpu.VMEM((ROWS, SLOTS), BF),
            pltpu.VMEM((C, SLOTS, W), BF),
            pltpu.VMEM((C, SLOTS, W), BF),
            pltpu.VMEM((SLOTS, D), F32),
            pltpu.VMEM((SLOTS, D), BF),
            dma((GROUPS,)), dma((GROUPS,)),
            dma((2, C, GROUPS)), dma((2, C, GROUPS)),
            dma((2, C)), dma((2, C)),
            dma((2, C, ZN)), dma((2, C, ZN)),
            dma((2, C, ZN)), dma((2, C, ZN)),
            dma((2, C, 20)), dma((2, C, 20)),
            dma((2, C, GROUPS)), dma((2, C, GROUPS)),
        ],
        compiler_params=pltpu.CompilerParams(
            collective_id=0, has_side_effects=True, vmem_limit_bytes=60 * 1024 * 1024
        ),
    )(packed, codes, scol, item, tgt)
    return out


def solution(mesh):
    in_specs = (P(("own", "pair"), None), P(("own", "pair")), P(("own", "pair")))
    out_specs = (P(("own", "pair"), None), P(("own", "pair"), None))
    return jax.shard_map(
        per_device, mesh=mesh, in_specs=in_specs, out_specs=out_specs, check_vma=False
    )
```

```python
import functools

import jax
import jax.numpy as jnp
from jax import lax
from jax.experimental import pallas as pl
from jax.experimental.pallas import tpu as pltpu
from jax.sharding import PartitionSpec as P

ROWS = 1024
D = 512
GROUPS = 16
CAP = 128
QUAD = 4 * CAP
SLOTS = GROUPS * CAP
GCODES = 512
ITEMS_PER_CODE = 32
CHUNKS = 2
W = D // CHUNKS
HALF = GCODES // 2
ZN = 8
ZC = HALF // ZN
LAG = 5.0
BF = jnp.bfloat16
F32 = jnp.float32
I32 = jnp.int32
NT = (((1,), (1,)), ((), ()))
NEAR_FIRST = (1, 7, 2, 6, 3, 5, 4)
QUADS = (0, 1, 3, 2)


def iota(shape, dim):
    return lax.broadcasted_iota(I32, shape, dim)


def hot(mask):
    return jnp.where(mask, 1.0, 0.0).astype(BF)


def slots_of(codes):
    groups = [lax.shift_right_logical(k, 9) for k in codes]
    ones = jnp.concatenate(
        [jnp.where(iota((GROUPS, ROWS), 0) == g, 1.0, 0.0) for g in groups], axis=0
    )
    blocks = ROWS // CAP
    stack = jnp.concatenate([ones[:, b * CAP : (b + 1) * CAP] for b in range(blocks)], axis=0)
    before = hot(iota((CAP, CAP), 0) < iota((CAP, CAP), 1))
    within = jnp.dot(stack.astype(BF), before, preferred_element_type=F32)
    total = jnp.sum(stack, axis=1, keepdims=True)
    n = 2 * GROUPS
    prefix = jnp.zeros((n, 1), F32)
    out = [[], []]
    for b in range(blocks):
        part = slice(b * n, (b + 1) * n)
        rank = (within[part] + prefix) * stack[part]
        prefix = prefix + total[part]
        for l in range(2):
            r = jnp.sum(rank[l * GROUPS : (l + 1) * GROUPS], axis=0, keepdims=True)
            out[l].append(groups[l][:, b * CAP : (b + 1) * CAP] * CAP + r.astype(I32))
    return [jnp.concatenate(o, axis=1) for o in out]


def main_kernel(
    rows_in, code_one, code_two,
    final_out, near_out,
    packed1, packed2, codes_out, codes_in, scol, tgt2,
    got, acc, half_out, half_in, zpart, zin, table, move, back, secp, nearacc, nearp,
    code_s, code_r, a2a_s, a2a_r, hs, hr, rzs, rzr, azs, azr, xs, xr, ss, sr,
):
    own = lax.axis_index("own")
    me = lax.axis_index("pair")
    z, c = lax.div(own, 2), lax.rem(own, 2)
    y, x = lax.div(me, 4), lax.rem(me, 4)
    sib = z * 2 + (1 - c)

    def at(dy, dx):
        return lax.rem(y + dy, 4) * 4 + lax.rem(x + dx, 4)

    def zat(dz):
        return lax.rem(z + dz, ZN) * 2 + c

    barrier = pltpu.get_barrier_semaphore()

    def greet(o, p):
        pl.semaphore_signal(barrier, inc=1, device_id=(o, p), device_id_type=pl.DeviceIdType.MESH)

    for d in range(1, 16):
        greet(own, at(d // 4, d % 4))
    for dz in range(1, ZN):
        greet(zat(dz), me)
    greet(sib, me)

    started = []

    def copy(src, dst, s, r, o, p):
        return pltpu.make_async_remote_copy(
            src_ref=src, dst_ref=dst, send_sem=s, recv_sem=r,
            device_id=(o, p), device_id_type=pl.DeviceIdType.MESH,
        )

    def send(src, dst, s, r, o, p):
        k = copy(src, dst, s, r, o, p)
        k.start()
        started.append(k)

    def arrive(dst, s, r):
        copy(dst, dst, s, r, own, at(0, 1)).wait_recv()

    packs = (packed1, packed2)

    codes = [
        jnp.concatenate([ref[b : b + 1, :] for b in range(8)], axis=1)
        for ref in (code_one, code_two)
    ]
    target = slots_of(codes)
    item = iota((1, ROWS), 1)

    def place_of(l, oy):
        return hot(iota((QUAD, ROWS), 0) + oy * QUAD == target[l])

    def note_slots(l, oy, place):
        local = jnp.bitwise_and(codes[l], GCODES - 1)
        feats = jnp.concatenate(
            [
                lax.shift_right_logical(local, 4),
                jnp.bitwise_and(local, 15),
                lax.shift_right_logical(item, 5),
                jnp.bitwise_and(item, 31),
                jnp.ones_like(item),
                jnp.zeros((3, ROWS), I32),
            ],
            axis=0,
        ).astype(F32).astype(BF)
        v = lax.dot_general(feats, place, NT, preferred_element_type=F32)
        dead = v[4:5] - 1.0
        vals = jnp.concatenate(
            [
                v[0:1] * 16.0 + v[1:2] + dead,
                v[2:3] * 32.0 + v[3:4] + dead * (1.0 + l),
                jnp.zeros((6, QUAD), F32),
            ],
            axis=0,
        )
        ints = vals.astype(I32)
        for j in range(4):
            codes_out[l, oy * 4 + j] = ints[:, j * CAP : (j + 1) * CAP]
        scol[l, pl.ds(pl.multiple_of(oy * QUAD, QUAD), QUAD), :] = jnp.transpose(vals).astype(I32)

    def send_codes(l, dy, dx):
        d, to = dy * 4 + dx, at(dy, dx)
        send(codes_out.at[l, to], codes_in.at[l, d], code_s.at[l, d], code_r.at[l, d], own, to)

    def send_rows(l, ch, dy, dx):
        d, to = dy * 4 + dx, at(dy, dx)
        send(packs[l].at[ch, to], got.at[l, ch, d], a2a_s.at[l, ch, d], a2a_r.at[l, ch, d], own, to)

    def sum_rows(l, ch, q):
        if q == 0:
            got[l, ch, 0] = packs[l][ch, me]
        for d in range(4 * q, 4 * q + 4):
            if d:
                arrive(got.at[l, ch, d], a2a_s.at[l, ch, d], a2a_r.at[l, ch, d])
                if ch == 0:
                    arrive(codes_in.at[l, d], code_s.at[l, d], code_r.at[l, d])
        ks = jnp.concatenate([codes_in[l, d, 0:1, :] for d in range(4 * q, 4 * q + 4)], axis=1)
        pick = hot(iota((GCODES, QUAD), 0) == ks)
        part = jnp.dot(pick, got[l, ch, 4 * q : 4 * q + 4].reshape(QUAD, W), preferred_element_type=F32)
        if q == QUADS[0]:
            acc[ch] = part
        else:
            acc[ch] += part

    def exchange(l, ch):
        half_out[l, ch] = acc[ch, pl.ds(pl.multiple_of((1 - c) * HALF, HALF), HALF)].astype(BF)
        send(half_out.at[l, ch], half_in.at[l, ch], hs.at[l, ch], hr.at[l, ch], sib, me)

    def reduce_z(l, ch):
        arrive(half_in.at[l, ch], hs.at[l, ch], hr.at[l, ch])
        mine = pl.ds(pl.multiple_of(c * HALF, HALF), HALF)
        both = acc[ch, mine] + half_in[l, ch].astype(F32)
        acc[ch, mine] = both
        zpart[l, ch] = both.astype(BF)
        for dz in NEAR_FIRST:
            to = lax.rem(z + dz, ZN)
            send(zpart.at[l, ch, pl.ds(pl.multiple_of(to * ZC, ZC), ZC)], zin.at[l, ch, dz],
                 rzs.at[l, ch, dz], rzr.at[l, ch, dz], zat(dz), me)

    def gather_z(l, ch):
        total = acc[ch, pl.ds(pl.multiple_of(c * HALF + z * ZC, ZC), ZC)]
        for dz in NEAR_FIRST:
            arrive(zin.at[l, ch, dz], rzs.at[l, ch, dz], rzr.at[l, ch, dz])
            total += zin[l, ch, dz].astype(F32)
        mine = pl.ds(pl.multiple_of(z * ZC, ZC), ZC)
        table[l, ch, 0, c, mine, :] = (total * (1.0 / ITEMS_PER_CODE)).astype(BF)
        for dz in NEAR_FIRST:
            here = table.at[l, ch, 0, c, mine]
            send(here, here, azs.at[l, ch, dz], azr.at[l, ch, dz], zat(dz), me)

    def turn(da, db):
        return da * (1 - c) + db * c, db * (1 - c) + da * c

    def slot(da, db):
        dy, dx = turn(da, db)
        return dy * 4 + dx

    def side(da, db):
        dy, dx = turn(da, db)
        return at(dy, dx)

    def to_sibling(l, ch, da, db):
        here = table.at[l, ch, slot(da, db), c]
        u = da * 4 + db
        send(here, here, ss.at[l, ch, u], sr.at[l, ch, u], sib, me)

    def piece(l, ch, da, db, part):
        if part is None:
            return table.at[l, ch, slot(da, db), c]
        return table.at[l, ch, slot(da, db), c, pl.ds(part * (HALF // 2), HALF // 2)]

    def pass_on(l, ch, source, dest, k, step, part):
        send(piece(l, ch, *source, part), piece(l, ch, *dest, part), xs.at[l, ch, k], xr.at[l, ch, k],
             own, side(*step))

    def come(l, ch, dest, k, part=None):
        arrive(piece(l, ch, *dest, part), xs.at[l, ch, k], xr.at[l, ch, k])

    def second_axis(l, ch, da):
        pass_on(l, ch, (da, 0), (da, 1), 4 + 4 * da, (0, 1), None)
        pass_on(l, ch, (da, 0), (da, 3), 5 + 4 * da, (0, 3), None)

    def start_plane(l, ch):
        here = table.at[l, ch, 0, c, pl.ds(0, ZC)]
        for dz in NEAR_FIRST:
            arrive(here, azs.at[l, ch, dz], azr.at[l, ch, dz])
        pass_on(l, ch, (0, 0), (1, 0), 0, (1, 0), None)
        pass_on(l, ch, (0, 0), (3, 0), 1, (3, 0), None)
        second_axis(l, ch, 0)
        to_sibling(l, ch, 0, 0)

    def first_hop(l, ch, da):
        k = 0 if da == 1 else 1
        come(l, ch, (da, 0), k)
        pass_on(l, ch, (da, 0), (2, 0), 2 + k, (da, 0), k)
        second_axis(l, ch, da)
        to_sibling(l, ch, da, 0)

    def first_far(l, ch):
        come(l, ch, (2, 0), 2, 0)
        come(l, ch, (2, 0), 3, 1)
        second_axis(l, ch, 2)
        to_sibling(l, ch, 2, 0)

    def second_hop(l, ch, da):
        for k, db in ((0, 1), (1, 3)):
            come(l, ch, (da, db), 4 + 4 * da + k)
            pass_on(l, ch, (da, db), (da, 2), 6 + 4 * da + k, (0, db), k)
            to_sibling(l, ch, da, db)

    def second_far(l, ch, da):
        come(l, ch, (da, 2), 6 + 4 * da, 0)
        come(l, ch, (da, 2), 7 + 4 * da, 1)
        to_sibling(l, ch, da, 2)

    def plane(l, ch, use):
        yield 3.0
        first_hop(l, ch, 1)
        first_hop(l, ch, 3)
        yield 0.5
        second_hop(l, ch, 0)
        use(0, 0)
        yield 2.0
        first_far(l, ch)
        yield 0.5
        second_hop(l, ch, 1)
        use(1, 0)
        use(0, 1)
        yield 0.5
        second_hop(l, ch, 3)
        use(3, 0)
        use(0, 3)
        yield 0.5
        second_far(l, ch, 0)
        yield 2.0
        second_hop(l, ch, 2)
        use(1, 1)
        use(1, 3)
        yield 1.0
        second_far(l, ch, 1)
        use(3, 1)
        use(3, 3)
        yield 0.5
        second_far(l, ch, 3)
        use(2, 0)
        use(0, 2)
        yield 2.0
        second_far(l, ch, 2)
        for da, db in ((1, 2), (2, 1), (3, 2), (2, 3), (2, 2)):
            use(da, db)

    def ready(l, ch, da, db):
        u = db * 4 + da
        dy, dx = turn(da, db)
        s = dy * 4 + dx
        arrive(table.at[l, ch, s, 1 - c], ss.at[l, ch, u], sr.at[l, ch, u])
        o = at(4 - dy, 4 - dx)
        place = pl.ds(pl.multiple_of(o * CAP, CAP), CAP)
        pick = hot(iota((CAP, GCODES), 1) == scol[l, place, 0:1])
        cents = table[l, ch, s].reshape(GCODES, W)
        return o, place, cents, jnp.dot(pick, cents, preferred_element_type=F32)

    def use_one(ch, da, db):
        o, place, _, picked = ready(0, ch, da, db)
        secp[ch, place, :] = (packed1[ch, o].astype(F32) - picked).astype(BF)

    def use_two(ch, da, db):
        o, place, cents, picked = ready(1, ch, da, db)
        rows = packed2[ch, o]
        wide = rows.astype(F32)
        secp[ch, place, :] = (wide - picked).astype(BF)
        prods = lax.dot_general(rows, cents, NT, preferred_element_type=F32)
        sq = jnp.sum(wide * wide, axis=1, keepdims=True)
        cw = cents.astype(F32)
        cw = cw * cw
        top = cw.astype(BF)
        low = (cw - top.astype(F32)).astype(BF)
        ones = jnp.ones((8, W), BF)
        csq = lax.dot_general(ones, top, NT, preferred_element_type=F32)
        csq += lax.dot_general(ones, low, NT, preferred_element_type=F32)
        part = sq - 2.0 * prods + csq[0:1]
        if ch == 0:
            nearacc[place, :] = part
        elif ch < CHUNKS - 1:
            nearacc[place, :] += part
        else:
            nearp[place, :] = ((nearacc[place, :] + part) * (1.0 / D)).astype(BF)

    quads_out = (1, 3, 0, 2)
    for ch in range(CHUNKS):
        for dy in quads_out:
            oy = lax.rem(y + dy, 4)
            place = place_of(0, oy)
            if ch == 0:
                note_slots(0, oy, place)
            got_rows = jnp.dot(place, rows_in[:, ch * W : (ch + 1) * W], preferred_element_type=F32)
            packed1[ch, pl.ds(oy * 4, 4)] = got_rows.astype(BF).reshape(4, CAP, W)
            if ch == 0 and dy == quads_out[0]:
                pl.semaphore_wait(barrier, 15 + ZN - 1 + 1)
            for dx in (1, 3, 0, 2):
                if dy or dx:
                    if ch == 0:
                        send_codes(0, dy, dx)
                    send_rows(0, ch, dy, dx)
    codes_in[0, 0] = codes_out[0, me]

    for dy in quads_out:
        oy = lax.rem(y + dy, 4)
        note_slots(1, oy, place_of(1, oy))
        for dx in (1, 3, 0, 2):
            if dy or dx:
                send_codes(1, dy, dx)
    codes_in[1, 0] = codes_out[1, me]
    tgt2[...] = jnp.transpose(jnp.broadcast_to(target[1].astype(F32), (8, ROWS))).astype(I32)
    first_items = jnp.concatenate([codes_out[0, o, 1:2, :] for o in range(GROUPS)], axis=1)

    def build_move(o, carry):
        rows = pl.ds(pl.multiple_of(o * CAP, CAP), CAP)
        move[rows, :] = hot(first_items == scol[1, rows, 1:2])
        return carry

    lax.fori_loop(0, GROUPS, build_move, 0)

    def build_back(b, carry):
        rows = pl.ds(pl.multiple_of(b * CAP, CAP), CAP)
        back[rows, :] = hot(iota((CAP, SLOTS), 1) == tgt2[rows, 0:1])
        return carry

    lax.fori_loop(0, ROWS // CAP, build_back, 0)

    def chain(ch):
        for l in range(2):
            for q in QUADS:
                sum_rows(l, ch, q)
                yield 1.0
            exchange(l, ch)
            yield 2.0
            reduce_z(l, ch)
            yield 4.0
            gather_z(l, ch)
            yield 4.0
            start_plane(l, ch)
            if l == 0:
                yield from plane(0, ch, functools.partial(use_one, ch))
                for dy in quads_out:
                    oy = lax.rem(y + dy, 4)
                    rows = move[pl.ds(pl.multiple_of(oy * QUAD, QUAD), QUAD), :]
                    moved = jnp.dot(rows, secp[ch], preferred_element_type=F32).astype(BF)
                    packed2[ch, pl.ds(oy * 4, 4)] = moved.reshape(4, CAP, W)
                    for dx in (1, 3, 0, 2):
                        if dy or dx:
                            send_rows(1, ch, dy, dx)
                    yield 0.5
                yield 10.0
            else:
                yield from plane(1, ch, functools.partial(use_two, ch))
                for b in range(2):
                    rows = back[b * 512 : (b + 1) * 512, :]
                    out = jnp.dot(rows, secp[ch], preferred_element_type=F32).astype(BF)
                    final_out[b * 512 : (b + 1) * 512, ch * W : (ch + 1) * W] = out
                    yield 0.5

    chains = [[ch * LAG, ch, chain(ch)] for ch in range(CHUNKS)]
    while chains:
        first = min(chains, key=lambda k: (k[0], k[1]))
        pause = next(first[2], None)
        if pause is None:
            chains.remove(first)
        else:
            first[0] += pause

    for b in range(2):
        rows = back[b * 512 : (b + 1) * 512, :]
        near_out[b * 512 : (b + 1) * 512, :] = jnp.dot(rows, nearp[...], preferred_element_type=F32).astype(BF)
    for k in started:
        k.wait_send()


def per_device(residual, code_one, code_two):
    dma = pltpu.SemaphoreType.DMA
    C = CHUNKS
    vmem = pl.BlockSpec(memory_space=pltpu.VMEM)
    return pl.pallas_call(
        main_kernel,
        out_shape=(
            jax.ShapeDtypeStruct((ROWS, D), BF),
            jax.ShapeDtypeStruct((ROWS, D), BF),
        ),
        in_specs=[vmem] * 3,
        out_specs=(vmem, vmem),
        scratch_shapes=[
            pltpu.VMEM((C, GROUPS, CAP, W), BF),
            pltpu.VMEM((C, GROUPS, CAP, W), BF),
            pltpu.VMEM((2, GROUPS, 8, CAP), I32),
            pltpu.VMEM((2, GROUPS, 8, CAP), I32),
            pltpu.VMEM((2, SLOTS, 8), I32),
            pltpu.VMEM((ROWS, 8), I32),
            pltpu.VMEM((2, C, GROUPS, CAP, W), BF),
            pltpu.VMEM((C, GCODES, W), F32),
            pltpu.VMEM((2, C, HALF, W), BF),
            pltpu.VMEM((2, C, HALF, W), BF),
            pltpu.VMEM((2, C, HALF, W), BF),
            pltpu.VMEM((2, C, ZN, ZC, W), BF),
            pltpu.VMEM((2, C, GROUPS, 2, HALF, W), BF),
            pltpu.VMEM((SLOTS, SLOTS), BF),
            pltpu.VMEM((ROWS, SLOTS), BF),
            pltpu.VMEM((C, SLOTS, W), BF),
            pltpu.VMEM((SLOTS, D), F32),
            pltpu.VMEM((SLOTS, D), BF),
            dma((2, GROUPS)), dma((2, GROUPS)),
            dma((2, C, GROUPS)), dma((2, C, GROUPS)),
            dma((2, C)), dma((2, C)),
            dma((2, C, ZN)), dma((2, C, ZN)),
            dma((2, C, ZN)), dma((2, C, ZN)),
            dma((2, C, 20)), dma((2, C, 20)),
            dma((2, C, GROUPS)), dma((2, C, GROUPS)),
        ],
        compiler_params=pltpu.CompilerParams(
            collective_id=0, has_side_effects=True, vmem_limit_bytes=60 * 1024 * 1024
        ),
    )(residual, code_one.reshape(8, CAP), code_two.reshape(8, CAP))


def solution(mesh):
    in_specs = (P(("own", "pair"), None), P(("own", "pair")), P(("own", "pair")))
    out_specs = (P(("own", "pair"), None), P(("own", "pair"), None))
    return jax.shard_map(
        per_device, mesh=mesh, in_specs=in_specs, out_specs=out_specs, check_vma=False
    )
```

```python
import functools
import types

import jax
import jax.numpy as jnp
from jax import lax
from jax.experimental import pallas as pl
from jax.experimental.pallas import tpu as pltpu
from jax.sharding import PartitionSpec as P

ROWS = 1024
D = 512
GROUPS = 16
CAP = 128
QUAD = 4 * CAP
SLOTS = GROUPS * CAP
GCODES = 512
ITEMS_PER_CODE = 32
PLANE_COLS = ((0, 256), (256, 128))
RING_COLS = (384, 128)
PIECE = GCODES // 16
HALF = GCODES // 2
ZN = 8
ZC = HALF // ZN
LAGS = (0.0, 5.0, -3.0)
BF = jnp.bfloat16
F32 = jnp.float32
I32 = jnp.int32
NT = (((1,), (1,)), ((), ()))
NEAR_FIRST = (1, 7, 2, 6, 3, 5, 4)
QUADS = (0, 1, 3, 2)
RING_ORDER = (1, 15, 2, 14, 3, 13, 4, 12, 5, 11, 6, 10, 7, 9, 8)


def iota(shape, dim):
    return lax.broadcasted_iota(I32, shape, dim)


def hot(mask):
    return jnp.where(mask, 1.0, 0.0).astype(BF)


def slots_of(codes):
    groups = [lax.shift_right_logical(k, 9) for k in codes]
    ones = jnp.concatenate(
        [jnp.where(iota((GROUPS, ROWS), 0) == g, 1.0, 0.0) for g in groups], axis=0
    )
    blocks = ROWS // CAP
    stack = jnp.concatenate([ones[:, b * CAP : (b + 1) * CAP] for b in range(blocks)], axis=0)
    before = hot(iota((CAP, CAP), 0) < iota((CAP, CAP), 1))
    within = jnp.dot(stack.astype(BF), before, preferred_element_type=F32)
    total = jnp.sum(stack, axis=1, keepdims=True)
    n = 2 * GROUPS
    prefix = jnp.zeros((n, 1), F32)
    out = [[], []]
    for b in range(blocks):
        part = slice(b * n, (b + 1) * n)
        rank = (within[part] + prefix) * stack[part]
        prefix = prefix + total[part]
        for l in range(2):
            r = jnp.sum(rank[l * GROUPS : (l + 1) * GROUPS], axis=0, keepdims=True)
            out[l].append(groups[l][:, b * CAP : (b + 1) * CAP] * CAP + r.astype(I32))
    return [jnp.concatenate(o, axis=1) for o in out]


def pair_of(name, shape):
    dma = pltpu.SemaphoreType.DMA
    return {name + "s": dma(shape), name + "r": dma(shape)}


def plane_scratch(w):
    dma = pltpu.SemaphoreType.DMA
    return {
        "packed1": pltpu.VMEM((GROUPS, CAP, w), BF),
        "packed2": pltpu.VMEM((GROUPS, CAP, w), BF),
        "got": pltpu.VMEM((2, GROUPS, CAP, w), BF),
        "acc": pltpu.VMEM((GCODES, w), F32),
        "half_out": pltpu.VMEM((2, HALF, w), BF),
        "half_in": pltpu.VMEM((2, HALF, w), BF),
        "zpart": pltpu.VMEM((2, HALF, w), BF),
        "zin": pltpu.VMEM((2, ZN, ZC, w), BF),
        "table": pltpu.VMEM((2, GROUPS, 2, HALF, w), BF),
        "secp": pltpu.VMEM((SLOTS, w), BF),
        "a2a_s": dma((2, GROUPS)),
        "a2a_r": dma((2, GROUPS)),
        **pair_of("h", (2,)),
        **pair_of("rz", (2, ZN)),
        **pair_of("az", (2, ZN)),
        **pair_of("x", (2, 20)),
        **pair_of("s", (2, GROUPS)),
    }


def ring_scratch(w):
    dma = pltpu.SemaphoreType.DMA
    return {
        "packed1": pltpu.VMEM((GROUPS, CAP, w), BF),
        "packed2": pltpu.VMEM((GROUPS, CAP, w), BF),
        "got": pltpu.VMEM((2, GROUPS, CAP, w), BF),
        "acc": pltpu.VMEM((GCODES, w), F32),
        "psend": pltpu.VMEM((2, GCODES, w), BF),
        "pin": pltpu.VMEM((2, GROUPS, PIECE, w), BF),
        "table": pltpu.VMEM((2, ZN, 2, GCODES, w), BF),
        "secp": pltpu.VMEM((SLOTS, w), BF),
        "a2a_s": dma((2, GROUPS)),
        "a2a_r": dma((2, GROUPS)),
        **pair_of("rp", (2, GROUPS)),
        **pair_of("gp", (2, GROUPS)),
        **pair_of("z", (2, ZN)),
        **pair_of("s", (2, ZN)),
    }


def main_kernel(
    rows_in, code_one, code_two,
    final_out, near_out,
    codes_out, codes_in, codes_ring, scol, tgt2, move, back, nearacc, nearp,
    code_s, code_r, ring_s, ring_r,
    *refs,
):
    own = lax.axis_index("own")
    me = lax.axis_index("pair")
    z, c = lax.div(own, 2), lax.rem(own, 2)
    y, x = lax.div(me, 4), lax.rem(me, 4)
    sib = z * 2 + (1 - c)
    refs = list(refs)
    chunks = []
    for cols in PLANE_COLS + (RING_COLS,):
        names = list(plane_scratch(cols[1]) if cols is not RING_COLS else ring_scratch(cols[1]))
        k = types.SimpleNamespace(**dict(zip(names, refs[: len(names)])))
        refs = refs[len(names) :]
        k.first, k.W, k.ring = cols[0], cols[1], cols is RING_COLS
        chunks.append(k)
    planes, ring = chunks[:-1], chunks[-1]

    def at(dy, dx):
        return lax.rem(y + dy, 4) * 4 + lax.rem(x + dx, 4)

    def zat(dz):
        return lax.rem(z + dz, ZN) * 2 + c

    barrier = pltpu.get_barrier_semaphore()

    def greet(o, p):
        pl.semaphore_signal(barrier, inc=1, device_id=(o, p), device_id_type=pl.DeviceIdType.MESH)

    for d in range(1, 16):
        greet(own, at(d // 4, d % 4))
    for d in range(1, 16):
        greet(lax.rem(own + d, 16), me)

    started = []

    def copy(src, dst, s, r, o, p):
        return pltpu.make_async_remote_copy(
            src_ref=src, dst_ref=dst, send_sem=s, recv_sem=r,
            device_id=(o, p), device_id_type=pl.DeviceIdType.MESH,
        )

    def send(src, dst, s, r, o, p):
        k = copy(src, dst, s, r, o, p)
        k.start()
        started.append(k)

    def arrive(dst, s, r):
        copy(dst, dst, s, r, own, at(0, 1)).wait_recv()

    def packs(k, l):
        return k.packed2 if l else k.packed1

    codes = [
        jnp.concatenate([ref[b : b + 1, :] for b in range(8)], axis=1)
        for ref in (code_one, code_two)
    ]
    target = slots_of(codes)
    item = iota((1, ROWS), 1)

    def place_of(l, oy):
        return hot(iota((QUAD, ROWS), 0) + oy * QUAD == target[l])

    def note_slots(l, oy, place):
        local = jnp.bitwise_and(codes[l], GCODES - 1)
        feats = jnp.concatenate(
            [
                lax.shift_right_logical(local, 4),
                jnp.bitwise_and(local, 15),
                lax.shift_right_logical(item, 5),
                jnp.bitwise_and(item, 31),
                jnp.ones_like(item),
                jnp.zeros((3, ROWS), I32),
            ],
            axis=0,
        ).astype(F32).astype(BF)
        v = lax.dot_general(feats, place, NT, preferred_element_type=F32)
        dead = v[4:5] - 1.0
        vals = jnp.concatenate(
            [
                v[0:1] * 16.0 + v[1:2] + dead,
                v[2:3] * 32.0 + v[3:4] + dead * (1.0 + l),
                jnp.zeros((6, QUAD), F32),
            ],
            axis=0,
        )
        ints = vals.astype(I32)
        for j in range(4):
            codes_out[l, oy * 4 + j] = ints[:, j * CAP : (j + 1) * CAP]
        scol[l, pl.ds(pl.multiple_of(oy * QUAD, QUAD), QUAD), :] = jnp.transpose(vals).astype(I32)

    def send_codes(l, dy, dx):
        d, to = dy * 4 + dx, at(dy, dx)
        send(codes_out.at[l, to], codes_in.at[l, d], code_s.at[l, d], code_r.at[l, d], own, to)

    def send_codes_ring(l):
        for d in RING_ORDER:
            to = lax.rem(own + d, 16)
            send(codes_out.at[l, to], codes_ring.at[l, d], ring_s.at[l, d], ring_r.at[l, d], to, me)

    def send_rows(l, ch, dy, dx):
        d, to = dy * 4 + dx, at(dy, dx)
        send(packs(ch, l).at[to], ch.got.at[l, d], ch.a2a_s.at[l, d], ch.a2a_r.at[l, d], own, to)

    def send_rows_ring(l):
        for d in RING_ORDER:
            to = lax.rem(own + d, 16)
            send(packs(ring, l).at[to], ring.got.at[l, d], ring.a2a_s.at[l, d], ring.a2a_r.at[l, d], to, me)

    def sum_rows(l, ch, q):
        if q == 0:
            ch.got[l, 0] = packs(ch, l)[own if ch.ring else me]
        known, ks, kr = (codes_ring, ring_s, ring_r) if ch.ring else (codes_in, code_s, code_r)
        for d in range(4 * q, 4 * q + 4):
            if d and (ch is planes[0] or ch.ring):
                arrive(known.at[l, d], ks.at[l, d], kr.at[l, d])
        lanes = jnp.concatenate([known[l, d, 0:1, :] for d in range(4 * q, 4 * q + 4)], axis=1)
        pick = hot(iota((GCODES, QUAD), 0) == lanes)
        for d in range(4 * q, 4 * q + 4):
            if d:
                arrive(ch.got.at[l, d], ch.a2a_s.at[l, d], ch.a2a_r.at[l, d])
        part = jnp.dot(pick, ch.got[l, 4 * q : 4 * q + 4].reshape(QUAD, ch.W), preferred_element_type=F32)
        if q == QUADS[0]:
            ch.acc[...] = part
        else:
            ch.acc[...] += part

    def exchange(l, ch):
        ch.half_out[l] = ch.acc[pl.ds(pl.multiple_of((1 - c) * HALF, HALF), HALF)].astype(BF)
        send(ch.half_out.at[l], ch.half_in.at[l], ch.hs.at[l], ch.hr.at[l], sib, me)

    def reduce_z(l, ch):
        arrive(ch.half_in.at[l], ch.hs.at[l], ch.hr.at[l])
        mine = pl.ds(pl.multiple_of(c * HALF, HALF), HALF)
        both = ch.acc[mine] + ch.half_in[l].astype(F32)
        ch.acc[mine] = both
        ch.zpart[l] = both.astype(BF)
        for dz in NEAR_FIRST:
            to = lax.rem(z + dz, ZN)
            send(ch.zpart.at[l, pl.ds(pl.multiple_of(to * ZC, ZC), ZC)], ch.zin.at[l, dz],
                 ch.rzs.at[l, dz], ch.rzr.at[l, dz], zat(dz), me)

    def gather_z(l, ch):
        total = ch.acc[pl.ds(pl.multiple_of(c * HALF + z * ZC, ZC), ZC)]
        for dz in NEAR_FIRST:
            arrive(ch.zin.at[l, dz], ch.rzs.at[l, dz], ch.rzr.at[l, dz])
            total += ch.zin[l, dz].astype(F32)
        mine = pl.ds(pl.multiple_of(z * ZC, ZC), ZC)
        ch.table[l, 0, c, mine, :] = (total * (1.0 / ITEMS_PER_CODE)).astype(BF)
        for dz in NEAR_FIRST:
            here = ch.table.at[l, 0, c, mine]
            send(here, here, ch.azs.at[l, dz], ch.azr.at[l, dz], zat(dz), me)

    def turn(da, db):
        return da * (1 - c) + db * c, db * (1 - c) + da * c

    def slot(da, db):
        dy, dx = turn(da, db)
        return dy * 4 + dx

    def side(da, db):
        dy, dx = turn(da, db)
        return at(dy, dx)

    def to_sibling(l, ch, da, db):
        here = ch.table.at[l, slot(da, db), c]
        u = da * 4 + db
        send(here, here, ch.ss.at[l, u], ch.sr.at[l, u], sib, me)

    def piece(l, ch, da, db, part):
        if part is None:
            return ch.table.at[l, slot(da, db), c]
        return ch.table.at[l, slot(da, db), c, pl.ds(part * (HALF // 2), HALF // 2)]

    def pass_on(l, ch, source, dest, k, step, part):
        send(piece(l, ch, *source, part), piece(l, ch, *dest, part), ch.xs.at[l, k], ch.xr.at[l, k],
             own, side(*step))

    def come(l, ch, dest, k, part=None):
        arrive(piece(l, ch, *dest, part), ch.xs.at[l, k], ch.xr.at[l, k])

    def second_axis(l, ch, da):
        pass_on(l, ch, (da, 0), (da, 1), 4 + 4 * da, (0, 1), None)
        pass_on(l, ch, (da, 0), (da, 3), 5 + 4 * da, (0, 3), None)

    def start_plane(l, ch):
        here = ch.table.at[l, 0, c, pl.ds(0, ZC)]
        for dz in NEAR_FIRST:
            arrive(here, ch.azs.at[l, dz], ch.azr.at[l, dz])
        pass_on(l, ch, (0, 0), (1, 0), 0, (1, 0), None)
        pass_on(l, ch, (0, 0), (3, 0), 1, (3, 0), None)
        second_axis(l, ch, 0)
        to_sibling(l, ch, 0, 0)

    def first_hop(l, ch, da):
        k = 0 if da == 1 else 1
        come(l, ch, (da, 0), k)
        pass_on(l, ch, (da, 0), (2, 0), 2 + k, (da, 0), k)
        second_axis(l, ch, da)
        to_sibling(l, ch, da, 0)

    def first_far(l, ch):
        come(l, ch, (2, 0), 2, 0)
        come(l, ch, (2, 0), 3, 1)
        second_axis(l, ch, 2)
        to_sibling(l, ch, 2, 0)

    def second_hop(l, ch, da):
        for k, db in ((0, 1), (1, 3)):
            come(l, ch, (da, db), 4 + 4 * da + k)
            pass_on(l, ch, (da, db), (da, 2), 6 + 4 * da + k, (0, db), k)
            to_sibling(l, ch, da, db)

    def second_far(l, ch, da):
        come(l, ch, (da, 2), 6 + 4 * da, 0)
        come(l, ch, (da, 2), 7 + 4 * da, 1)
        to_sibling(l, ch, da, 2)

    def plane(l, ch, use):
        yield 3.0
        first_hop(l, ch, 1)
        first_hop(l, ch, 3)
        yield 0.5
        second_hop(l, ch, 0)
        use(0, 0)
        yield 2.0
        first_far(l, ch)
        yield 0.5
        second_hop(l, ch, 1)
        use(1, 0)
        use(0, 1)
        yield 0.5
        second_hop(l, ch, 3)
        use(3, 0)
        use(0, 3)
        yield 0.5
        second_far(l, ch, 0)
        yield 2.0
        second_hop(l, ch, 2)
        use(1, 1)
        use(1, 3)
        yield 1.0
        second_far(l, ch, 1)
        use(3, 1)
        use(3, 3)
        yield 0.5
        second_far(l, ch, 3)
        use(2, 0)
        use(0, 2)
        yield 1.5
        for da, db in ((1, 2), (2, 1), (3, 2), (2, 3)):
            use(da, db)
        yield 0.5
        second_far(l, ch, 2)
        use(2, 2)

    def ready(l, ch, da, db):
        u = db * 4 + da
        dy, dx = turn(da, db)
        s = dy * 4 + dx
        arrive(ch.table.at[l, s, 1 - c], ch.ss.at[l, u], ch.sr.at[l, u])
        o = at(4 - dy, 4 - dx)
        place = pl.ds(pl.multiple_of(o * CAP, CAP), CAP)
        pick = hot(iota((CAP, GCODES), 1) == scol[l, place, 0:1])
        cents = ch.table[l, s].reshape(GCODES, ch.W)
        return o, place, cents, jnp.dot(pick, cents, preferred_element_type=F32)

    def use_one(ch, *where):
        o, place, _, picked = (ready_ring if ch.ring else ready)(0, ch, *where)
        ch.secp[place, :] = (ch.packed1[o].astype(F32) - picked).astype(BF)

    def use_two(ch, *where):
        o, place, cents, picked = (ready_ring if ch.ring else ready)(1, ch, *where)
        rows = ch.packed2[o]
        wide = rows.astype(F32)
        ch.secp[place, :] = (wide - picked).astype(BF)
        prods = lax.dot_general(rows, cents, NT, preferred_element_type=F32)
        sq = jnp.sum(wide * wide, axis=1, keepdims=True)
        cw = cents.astype(F32)
        cw = cw * cw
        top = cw.astype(BF)
        low = (cw - top.astype(F32)).astype(BF)
        ones = jnp.ones((8, ch.W), BF)
        csq = lax.dot_general(ones, top, NT, preferred_element_type=F32)
        csq += lax.dot_general(ones, low, NT, preferred_element_type=F32)
        nearacc[place, :] += sq - 2.0 * prods + csq[0:1]

    far_last = [(0, 1), (1, 0), (0, 3), (3, 0), (1, 1), (3, 3), (1, 3), (3, 1),
                (0, 2), (2, 0), (1, 2), (2, 1), (3, 2), (2, 3), (2, 2)]

    def piece_of(p):
        return pl.ds(pl.multiple_of(p * PIECE, PIECE), PIECE)

    def reduce_plane(l):
        ring.psend[l] = ring.acc[...].astype(BF)
        for dy, dx in far_last:
            d, to = dy * 4 + dx, at(dy, dx)
            send(ring.psend.at[l, piece_of(to)], ring.pin.at[l, d], ring.rps.at[l, d], ring.rpr.at[l, d], own, to)

    def gather_plane(l):
        total = ring.acc[piece_of(me)]
        for dy, dx in far_last:
            d = dy * 4 + dx
            arrive(ring.pin.at[l, d], ring.rps.at[l, d], ring.rpr.at[l, d])
            total += ring.pin[l, d].astype(F32)
        ring.table[l, 0, c, piece_of(me), :] = (total * (1.0 / ITEMS_PER_CODE)).astype(BF)
        here = ring.table.at[l, 0, c, piece_of(me)]
        for dy, dx in far_last:
            d = dy * 4 + dx
            send(here, here, ring.gps.at[l, d], ring.gpr.at[l, d], own, at(dy, dx))

    def ring_pass(l, source, dest, up, part):
        if part is None:
            a, b, n = ring.table.at[l, source, c], ring.table.at[l, dest, c], dest
        else:
            half = pl.ds(part * HALF, HALF)
            a, b, n = ring.table.at[l, source, c, half], ring.table.at[l, dest, c, half], 4 * (1 - part)
        send(a, b, ring.zs.at[l, n], ring.zr.at[l, n], zat(1 if up else ZN - 1), me)

    def ring_sibling(l, dz):
        here = ring.table.at[l, dz, c]
        send(here, here, ring.ss.at[l, dz], ring.sr.at[l, dz], sib, me)

    def ring_start(l):
        here = ring.table.at[l, 0, c, pl.ds(0, PIECE)]
        for dy, dx in far_last:
            d = dy * 4 + dx
            arrive(here, ring.gps.at[l, d], ring.gpr.at[l, d])
        ring_pass(l, 0, 1, True, None)
        ring_pass(l, 0, 7, False, None)
        ring_sibling(l, 0)

    def ring_hop(l, dz):
        arrive(ring.table.at[l, dz, c], ring.zs.at[l, dz], ring.zr.at[l, dz])
        up = dz < 4
        to = dz + 1 if up else dz - 1
        ring_pass(l, dz, to, up, (0 if up else 1) if to == 4 else None)
        ring_sibling(l, dz)

    def ring_far(l):
        for part in range(2):
            n = 4 * (1 - part)
            arrive(ring.table.at[l, 4, c, pl.ds(part * HALF, HALF)], ring.zs.at[l, n], ring.zr.at[l, n])
        ring_sibling(l, 4)

    def ready_ring(l, ch, dz, other):
        if other:
            arrive(ring.table.at[l, dz, 1 - c], ring.ss.at[l, dz], ring.sr.at[l, dz])
            cc = 1 - c
        else:
            cc = c
        o = lax.rem(z + ZN - dz, ZN) * 2 + cc
        place = pl.ds(pl.multiple_of(o * CAP, CAP), CAP)
        pick = hot(iota((CAP, GCODES), 1) == scol[l, place, 0:1])
        cents = ring.table[l, dz, cc]
        return o, place, cents, jnp.dot(pick, cents, preferred_element_type=F32)

    def ring_all(l, use):
        use(0, False)
        yield 2.0
        for up in (1, 2, 3):
            ring_hop(l, up)
            ring_hop(l, ZN - up)
            yield 1.5
            use((up - 1), True)
            if up > 1:
                use(ZN - up + 1, True)
            use(up, False)
            use(ZN - up, False)
            yield 2.5
        ring_far(l)
        for dz, other in ((3, True), (5, True), (4, False)):
            use(dz, other)
        yield 1.5
        use(4, True)

    quads_out = (1, 3, 0, 2)

    def pack(ch, oy, place):
        cols = rows_in[:, ch.first : ch.first + ch.W]
        moved = jnp.dot(place, cols, preferred_element_type=F32).astype(BF)
        ch.packed1[pl.ds(oy * 4, 4)] = moved.reshape(4, CAP, ch.W)

    for n, ch in enumerate((planes[0], ring, planes[1])):
        for dy in quads_out:
            oy = lax.rem(y + dy, 4)
            place = place_of(0, oy)
            if n == 0:
                note_slots(0, oy, place)
            pack(ch, oy, place)
            if n == 0 and dy == quads_out[0]:
                pl.semaphore_wait(barrier, 30)
            for dx in (1, 3, 0, 2):
                if (dy or dx) and not ch.ring:
                    if n == 0:
                        send_codes(0, dy, dx)
                    send_rows(0, ch, dy, dx)
        if ch.ring:
            send_codes_ring(0)
            send_rows_ring(0)
    codes_in[0, 0] = codes_out[0, me]
    codes_ring[0, 0] = codes_out[0, own]

    for dy in quads_out:
        oy = lax.rem(y + dy, 4)
        note_slots(1, oy, place_of(1, oy))
        for dx in (1, 3, 0, 2):
            if dy or dx:
                send_codes(1, dy, dx)
    send_codes_ring(1)
    codes_in[1, 0] = codes_out[1, me]
    codes_ring[1, 0] = codes_out[1, own]
    nearacc[...] = jnp.zeros_like(nearacc)
    tgt2[...] = jnp.transpose(jnp.broadcast_to(target[1].astype(F32), (8, ROWS))).astype(I32)
    first_items = jnp.concatenate([codes_out[0, o, 1:2, :] for o in range(GROUPS)], axis=1)

    def build_move(o, carry):
        rows = pl.ds(pl.multiple_of(o * CAP, CAP), CAP)
        move[rows, :] = hot(first_items == scol[1, rows, 1:2])
        return carry

    lax.fori_loop(0, GROUPS, build_move, 0)

    def build_back(b, carry):
        rows = pl.ds(pl.multiple_of(b * CAP, CAP), CAP)
        back[rows, :] = hot(iota((CAP, SLOTS), 1) == tgt2[rows, 0:1])
        return carry

    lax.fori_loop(0, ROWS // CAP, build_back, 0)

    def move_rows(ch, oy):
        rows = move[pl.ds(pl.multiple_of(oy * QUAD, QUAD), QUAD), :]
        moved = jnp.dot(rows, ch.secp[...], preferred_element_type=F32).astype(BF)
        ch.packed2[pl.ds(oy * 4, 4)] = moved.reshape(4, CAP, ch.W)

    def finish(ch):
        for b in range(2):
            rows = back[b * 512 : (b + 1) * 512, :]
            out = jnp.dot(rows, ch.secp[...], preferred_element_type=F32).astype(BF)
            final_out[b * 512 : (b + 1) * 512, ch.first : ch.first + ch.W] = out

    def chain(ch):
        for l in range(2):
            for q in QUADS:
                sum_rows(l, ch, q)
                yield 1.0
            exchange(l, ch)
            yield 2.0
            reduce_z(l, ch)
            yield 4.0
            gather_z(l, ch)
            yield 4.0
            start_plane(l, ch)
            if l == 0:
                yield from plane(0, ch, functools.partial(use_one, ch))
                for dy in quads_out:
                    move_rows(ch, lax.rem(y + dy, 4))
                    for dx in (1, 3, 0, 2):
                        if dy or dx:
                            send_rows(1, ch, dy, dx)
                    yield 0.5
                yield 10.0
            else:
                yield from plane(1, ch, functools.partial(use_two, ch))
                finish(ch)

    def ring_chain():
        for l in range(2):
            for q in (0, 3, 1, 2):
                sum_rows(l, ring, q)
                yield 1.0
            reduce_plane(l)
            yield 5.0
            gather_plane(l)
            yield 4.0
            ring_start(l)
            yield 1.0
            yield from ring_all(l, functools.partial((use_one, use_two)[l], ring))
            if l == 0:
                for oy in range(4):
                    move_rows(ring, oy)
                    yield 0.5
                send_rows_ring(1)
                yield 12.0
            else:
                finish(ring)

    gens = [chain(planes[0]), chain(planes[1]), ring_chain()]
    chains = [[LAGS[n], n, g] for n, g in enumerate(gens)]
    while chains:
        first = min(chains, key=lambda k: (k[0], k[1]))
        pause = next(first[2], None)
        if pause is None:
            chains.remove(first)
        else:
            first[0] += pause

    def settle(b, carry):
        rows = pl.ds(pl.multiple_of(b * CAP, CAP), CAP)
        nearp[rows, :] = (nearacc[rows, :] * (1.0 / D)).astype(BF)
        return carry

    lax.fori_loop(0, GROUPS, settle, 0)
    for b in range(2):
        rows = back[b * 512 : (b + 1) * 512, :]
        near_out[b * 512 : (b + 1) * 512, :] = jnp.dot(rows, nearp[...], preferred_element_type=F32).astype(BF)
    for k in started:
        k.wait_send()


def per_device(residual, code_one, code_two):
    dma = pltpu.SemaphoreType.DMA
    vmem = pl.BlockSpec(memory_space=pltpu.VMEM)
    scratch = [
        pltpu.VMEM((2, GROUPS, 8, CAP), I32),
        pltpu.VMEM((2, GROUPS, 8, CAP), I32),
        pltpu.VMEM((2, GROUPS, 8, CAP), I32),
        pltpu.VMEM((2, SLOTS, 8), I32),
        pltpu.VMEM((ROWS, 8), I32),
        pltpu.VMEM((SLOTS, SLOTS), BF),
        pltpu.VMEM((ROWS, SLOTS), BF),
        pltpu.VMEM((SLOTS, D), F32),
        pltpu.VMEM((SLOTS, D), BF),
        dma((2, GROUPS)), dma((2, GROUPS)), dma((2, GROUPS)), dma((2, GROUPS)),
    ]
    for _, w in PLANE_COLS:
        scratch += list(plane_scratch(w).values())
    scratch += list(ring_scratch(RING_COLS[1]).values())
    return pl.pallas_call(
        main_kernel,
        out_shape=(
            jax.ShapeDtypeStruct((ROWS, D), BF),
            jax.ShapeDtypeStruct((ROWS, D), BF),
        ),
        in_specs=[vmem] * 3,
        out_specs=(vmem, vmem),
        scratch_shapes=scratch,
        compiler_params=pltpu.CompilerParams(
            collective_id=0, has_side_effects=True, vmem_limit_bytes=60 * 1024 * 1024
        ),
    )(residual, code_one.reshape(8, CAP), code_two.reshape(8, CAP))


def solution(mesh):
    in_specs = (P(("own", "pair"), None), P(("own", "pair")), P(("own", "pair")))
    out_specs = (P(("own", "pair"), None), P(("own", "pair"), None))
    return jax.shard_map(
        per_device, mesh=mesh, in_specs=in_specs, out_specs=out_specs, check_vma=False
    )
```

```python
import functools

import jax
import jax.numpy as jnp
from jax import lax
from jax.experimental import pallas as pl
from jax.experimental.pallas import tpu as pltpu
from jax.sharding import PartitionSpec as P

ROWS = 1024
D = 512
GROUPS = 16
CAP = 128
QUAD = 4 * CAP
SLOTS = GROUPS * CAP
GCODES = 512
ITEMS_PER_CODE = 32
CHUNKS = 2
W = D // CHUNKS
HALF = GCODES // 2
ZN = 8
ZC = HALF // ZN
LAG = 5.0
BF = jnp.bfloat16
F32 = jnp.float32
I32 = jnp.int32
NT = (((1,), (1,)), ((), ()))
NEAR_FIRST = (1, 7, 2, 6, 3, 5, 4)
QUADS = (0, 1, 3, 2)


def iota(shape, dim):
    return lax.broadcasted_iota(I32, shape, dim)


def hot(mask):
    return jnp.where(mask, 1.0, 0.0).astype(BF)


def slots_of(codes):
    groups = [lax.shift_right_logical(k, 9) for k in codes]
    ones = jnp.concatenate(
        [jnp.where(iota((GROUPS, ROWS), 0) == g, 1.0, 0.0) for g in groups], axis=0
    )
    blocks = ROWS // CAP
    stack = jnp.concatenate([ones[:, b * CAP : (b + 1) * CAP] for b in range(blocks)], axis=0)
    before = hot(iota((CAP, CAP), 0) < iota((CAP, CAP), 1))
    within = jnp.dot(stack.astype(BF), before, preferred_element_type=F32)
    total = jnp.sum(stack, axis=1, keepdims=True)
    n = 2 * GROUPS
    prefix = jnp.zeros((n, 1), F32)
    out = [[], []]
    for b in range(blocks):
        part = slice(b * n, (b + 1) * n)
        rank = (within[part] + prefix) * stack[part]
        prefix = prefix + total[part]
        for l in range(2):
            r = jnp.sum(rank[l * GROUPS : (l + 1) * GROUPS], axis=0, keepdims=True)
            out[l].append(groups[l][:, b * CAP : (b + 1) * CAP] * CAP + r.astype(I32))
    return [jnp.concatenate(o, axis=1) for o in out]


def main_kernel(
    rows_in, code_one, code_two,
    final_out, near_out,
    packed1, packed2, codes_out, codes_in, scol, tgt2,
    got, acc, half_out, half_in, zpart, zin, table, move, back, secp, nearacc, nearp,
    code_s, code_r, a2a_s, a2a_r, hs, hr, rzs, rzr, azs, azr, xs, xr, ss, sr,
):
    own = lax.axis_index("own")
    me = lax.axis_index("pair")
    z, c = lax.div(own, 2), lax.rem(own, 2)
    y, x = lax.div(me, 4), lax.rem(me, 4)
    sib = z * 2 + (1 - c)

    def at(dy, dx):
        return lax.rem(y + dy, 4) * 4 + lax.rem(x + dx, 4)

    def zat(dz):
        return lax.rem(z + dz, ZN) * 2 + c

    barrier = pltpu.get_barrier_semaphore()

    def greet(o, p):
        pl.semaphore_signal(barrier, inc=1, device_id=(o, p), device_id_type=pl.DeviceIdType.MESH)

    for d in range(1, 16):
        greet(own, at(d // 4, d % 4))
    for dz in range(1, ZN):
        greet(zat(dz), me)
    greet(sib, me)

    started = []

    def copy(src, dst, s, r, o, p):
        return pltpu.make_async_remote_copy(
            src_ref=src, dst_ref=dst, send_sem=s, recv_sem=r,
            device_id=(o, p), device_id_type=pl.DeviceIdType.MESH,
        )

    def send(src, dst, s, r, o, p):
        k = copy(src, dst, s, r, o, p)
        k.start()
        started.append(k)

    def arrive(dst, s, r):
        copy(dst, dst, s, r, own, at(0, 1)).wait_recv()

    packs = (packed1, packed2)

    codes = [
        jnp.concatenate([ref[b : b + 1, :] for b in range(8)], axis=1)
        for ref in (code_one, code_two)
    ]
    target = slots_of(codes)
    item = iota((1, ROWS), 1)

    def place_of(l, oy):
        return hot(iota((QUAD, ROWS), 0) + oy * QUAD == target[l])

    def note_slots(l, oy, place):
        local = jnp.bitwise_and(codes[l], GCODES - 1)
        feats = jnp.concatenate(
            [
                lax.shift_right_logical(local, 4),
                jnp.bitwise_and(local, 15),
                lax.shift_right_logical(item, 5),
                jnp.bitwise_and(item, 31),
                jnp.ones_like(item),
                jnp.zeros((3, ROWS), I32),
            ],
            axis=0,
        ).astype(F32).astype(BF)
        v = lax.dot_general(feats, place, NT, preferred_element_type=F32)
        dead = v[4:5] - 1.0
        vals = jnp.concatenate(
            [
                v[0:1] * 16.0 + v[1:2] + dead,
                v[2:3] * 32.0 + v[3:4] + dead * (1.0 + l),
                jnp.zeros((6, QUAD), F32),
            ],
            axis=0,
        )
        ints = vals.astype(I32)
        for j in range(4):
            codes_out[l, oy * 4 + j] = ints[:, j * CAP : (j + 1) * CAP]
        scol[l, pl.ds(pl.multiple_of(oy * QUAD, QUAD), QUAD), :] = jnp.transpose(vals).astype(I32)

    def send_codes(l, dy, dx):
        d, to = dy * 4 + dx, at(dy, dx)
        send(codes_out.at[l, to], codes_in.at[l, d], code_s.at[l, d], code_r.at[l, d], own, to)

    def send_rows(l, ch, dy, dx):
        d, to = dy * 4 + dx, at(dy, dx)
        send(packs[l].at[ch, to], got.at[l, ch, d], a2a_s.at[l, ch, d], a2a_r.at[l, ch, d], own, to)

    def sum_rows(l, ch, q):
        if q == 0:
            got[l, ch, 0] = packs[l][ch, me]
        for d in range(4 * q, 4 * q + 4):
            if d and ch == 0:
                arrive(codes_in.at[l, d], code_s.at[l, d], code_r.at[l, d])
        ks = jnp.concatenate([codes_in[l, d, 0:1, :] for d in range(4 * q, 4 * q + 4)], axis=1)
        pick = hot(iota((GCODES, QUAD), 0) == ks)
        for d in range(4 * q, 4 * q + 4):
            if d:
                arrive(got.at[l, ch, d], a2a_s.at[l, ch, d], a2a_r.at[l, ch, d])
        part = jnp.dot(pick, got[l, ch, 4 * q : 4 * q + 4].reshape(QUAD, W), preferred_element_type=F32)
        if q == QUADS[0]:
            acc[ch] = part
        else:
            acc[ch] += part

    def exchange(l, ch):
        half_out[l, ch] = acc[ch, pl.ds(pl.multiple_of((1 - c) * HALF, HALF), HALF)].astype(BF)
        send(half_out.at[l, ch], half_in.at[l, ch], hs.at[l, ch], hr.at[l, ch], sib, me)

    def reduce_z(l, ch):
        arrive(half_in.at[l, ch], hs.at[l, ch], hr.at[l, ch])
        mine = pl.ds(pl.multiple_of(c * HALF, HALF), HALF)
        both = acc[ch, mine] + half_in[l, ch].astype(F32)
        acc[ch, mine] = both
        zpart[l, ch] = both.astype(BF)
        for dz in NEAR_FIRST:
            to = lax.rem(z + dz, ZN)
            send(zpart.at[l, ch, pl.ds(pl.multiple_of(to * ZC, ZC), ZC)], zin.at[l, ch, dz],
                 rzs.at[l, ch, dz], rzr.at[l, ch, dz], zat(dz), me)

    def gather_z(l, ch):
        total = acc[ch, pl.ds(pl.multiple_of(c * HALF + z * ZC, ZC), ZC)]
        for dz in NEAR_FIRST:
            arrive(zin.at[l, ch, dz], rzs.at[l, ch, dz], rzr.at[l, ch, dz])
            total += zin[l, ch, dz].astype(F32)
        mine = pl.ds(pl.multiple_of(z * ZC, ZC), ZC)
        table[l, ch, 0, c, mine, :] = (total * (1.0 / ITEMS_PER_CODE)).astype(BF)
        for dz in NEAR_FIRST:
            here = table.at[l, ch, 0, c, mine]
            send(here, here, azs.at[l, ch, dz], azr.at[l, ch, dz], zat(dz), me)

    def turn(da, db):
        return da * (1 - c) + db * c, db * (1 - c) + da * c

    def slot(da, db):
        dy, dx = turn(da, db)
        return dy * 4 + dx

    def side(da, db):
        dy, dx = turn(da, db)
        return at(dy, dx)

    def to_sibling(l, ch, da, db):
        here = table.at[l, ch, slot(da, db), c]
        u = da * 4 + db
        send(here, here, ss.at[l, ch, u], sr.at[l, ch, u], sib, me)

    def piece(l, ch, da, db, part):
        if part is None:
            return table.at[l, ch, slot(da, db), c]
        return table.at[l, ch, slot(da, db), c, pl.ds(part * (HALF // 2), HALF // 2)]

    def pass_on(l, ch, source, dest, k, step, part):
        send(piece(l, ch, *source, part), piece(l, ch, *dest, part), xs.at[l, ch, k], xr.at[l, ch, k],
             own, side(*step))

    def come(l, ch, dest, k, part=None):
        arrive(piece(l, ch, *dest, part), xs.at[l, ch, k], xr.at[l, ch, k])

    def second_axis(l, ch, da):
        pass_on(l, ch, (da, 0), (da, 1), 4 + 4 * da, (0, 1), None)
        pass_on(l, ch, (da, 0), (da, 3), 5 + 4 * da, (0, 3), None)

    def start_plane(l, ch):
        here = table.at[l, ch, 0, c, pl.ds(0, ZC)]
        for dz in NEAR_FIRST:
            arrive(here, azs.at[l, ch, dz], azr.at[l, ch, dz])
        pass_on(l, ch, (0, 0), (1, 0), 0, (1, 0), None)
        pass_on(l, ch, (0, 0), (3, 0), 1, (3, 0), None)
        second_axis(l, ch, 0)
        to_sibling(l, ch, 0, 0)

    def first_hop(l, ch, da):
        k = 0 if da == 1 else 1
        come(l, ch, (da, 0), k)
        pass_on(l, ch, (da, 0), (2, 0), 2 + k, (da, 0), k)
        second_axis(l, ch, da)
        to_sibling(l, ch, da, 0)

    def first_far(l, ch):
        come(l, ch, (2, 0), 2, 0)
        come(l, ch, (2, 0), 3, 1)
        second_axis(l, ch, 2)
        to_sibling(l, ch, 2, 0)

    def second_hop(l, ch, da):
        for k, db in ((0, 1), (1, 3)):
            come(l, ch, (da, db), 4 + 4 * da + k)
            pass_on(l, ch, (da, db), (da, 2), 6 + 4 * da + k, (0, db), k)
            to_sibling(l, ch, da, db)

    def second_far(l, ch, da):
        come(l, ch, (da, 2), 6 + 4 * da, 0)
        come(l, ch, (da, 2), 7 + 4 * da, 1)
        to_sibling(l, ch, da, 2)

    def plane(l, ch, use):
        yield 3.0
        first_hop(l, ch, 1)
        first_hop(l, ch, 3)
        yield 0.5
        second_hop(l, ch, 0)
        use(0, 0)
        yield 2.0
        first_far(l, ch)
        yield 0.5
        second_hop(l, ch, 1)
        use(1, 0)
        use(0, 1)
        yield 0.5
        second_hop(l, ch, 3)
        use(3, 0)
        use(0, 3)
        yield 0.5
        second_far(l, ch, 0)
        yield 2.0
        second_hop(l, ch, 2)
        use(1, 1)
        use(1, 3)
        yield 1.0
        second_far(l, ch, 1)
        use(3, 1)
        use(3, 3)
        yield 0.5
        second_far(l, ch, 3)
        use(2, 0)
        use(0, 2)
        yield 1.5
        for da, db in ((1, 2), (2, 1), (3, 2), (2, 3)):
            use(da, db)
        yield 0.5
        second_far(l, ch, 2)
        use(2, 2)

    def ready(l, ch, da, db):
        u = db * 4 + da
        dy, dx = turn(da, db)
        s = dy * 4 + dx
        o = at(4 - dy, 4 - dx)
        place = pl.ds(pl.multiple_of(o * CAP, CAP), CAP)
        pick = hot(iota((CAP, GCODES), 1) == scol[l, place, 0:1])
        arrive(table.at[l, ch, s, 1 - c], ss.at[l, ch, u], sr.at[l, ch, u])
        cents = table[l, ch, s].reshape(GCODES, W)
        return o, place, cents, jnp.dot(pick, cents, preferred_element_type=F32)

    def use_one(ch, da, db):
        o, place, _, picked = ready(0, ch, da, db)
        secp[ch, place, :] = (packed1[ch, o].astype(F32) - picked).astype(BF)

    def use_two(ch, da, db):
        o, place, cents, picked = ready(1, ch, da, db)
        rows = packed2[ch, o]
        wide = rows.astype(F32)
        secp[ch, place, :] = (wide - picked).astype(BF)
        prods = lax.dot_general(rows, cents, NT, preferred_element_type=F32)
        sq = jnp.sum(wide * wide, axis=1, keepdims=True)
        cw = cents.astype(F32)
        cw = cw * cw
        top = cw.astype(BF)
        low = (cw - top.astype(F32)).astype(BF)
        ones = jnp.ones((8, W), BF)
        csq = lax.dot_general(ones, top, NT, preferred_element_type=F32)
        csq += lax.dot_general(ones, low, NT, preferred_element_type=F32)
        part = sq - 2.0 * prods + csq[0:1]
        if ch == 0:
            nearacc[place, :] = part
        elif ch < CHUNKS - 1:
            nearacc[place, :] += part
        else:
            nearp[place, :] = ((nearacc[place, :] + part) * (1.0 / D)).astype(BF)

    quads_out = (1, 3, 0, 2)
    for ch in range(CHUNKS):
        for dy in quads_out:
            oy = lax.rem(y + dy, 4)
            place = place_of(0, oy)
            if ch == 0:
                note_slots(0, oy, place)
            got_rows = jnp.dot(place, rows_in[:, ch * W : (ch + 1) * W], preferred_element_type=F32)
            packed1[ch, pl.ds(oy * 4, 4)] = got_rows.astype(BF).reshape(4, CAP, W)
            if ch == 0 and dy == quads_out[0]:
                pl.semaphore_wait(barrier, 15 + ZN - 1 + 1)
            for dx in (1, 3, 0, 2):
                if dy or dx:
                    if ch == 0:
                        send_codes(0, dy, dx)
                    send_rows(0, ch, dy, dx)
    codes_in[0, 0] = codes_out[0, me]

    for dy in quads_out:
        oy = lax.rem(y + dy, 4)
        note_slots(1, oy, place_of(1, oy))
        for dx in (1, 3, 0, 2):
            if dy or dx:
                send_codes(1, dy, dx)
    codes_in[1, 0] = codes_out[1, me]
    tgt2[...] = jnp.transpose(jnp.broadcast_to(target[1].astype(F32), (8, ROWS))).astype(I32)
    first_items = jnp.concatenate([codes_out[0, o, 1:2, :] for o in range(GROUPS)], axis=1)

    def build_move(o, carry):
        rows = pl.ds(pl.multiple_of(o * CAP, CAP), CAP)
        move[rows, :] = hot(first_items == scol[1, rows, 1:2])
        return carry

    lax.fori_loop(0, GROUPS, build_move, 0)

    def build_back(b, carry):
        rows = pl.ds(pl.multiple_of(b * CAP, CAP), CAP)
        back[rows, :] = hot(iota((CAP, SLOTS), 1) == tgt2[rows, 0:1])
        return carry

    lax.fori_loop(0, ROWS // CAP, build_back, 0)

    def chain(ch):
        for l in range(2):
            for q in QUADS:
                sum_rows(l, ch, q)
                yield 1.0
            exchange(l, ch)
            yield 2.0
            reduce_z(l, ch)
            yield 4.0
            gather_z(l, ch)
            yield 4.0
            start_plane(l, ch)
            if l == 0:
                yield from plane(0, ch, functools.partial(use_one, ch))
                for dy in quads_out:
                    oy = lax.rem(y + dy, 4)
                    rows = move[pl.ds(pl.multiple_of(oy * QUAD, QUAD), QUAD), :]
                    moved = jnp.dot(rows, secp[ch], preferred_element_type=F32).astype(BF)
                    packed2[ch, pl.ds(oy * 4, 4)] = moved.reshape(4, CAP, W)
                    for dx in (1, 3, 0, 2):
                        if dy or dx:
                            send_rows(1, ch, dy, dx)
                    yield 0.5
                yield 10.0
            else:
                yield from plane(1, ch, functools.partial(use_two, ch))
                for b in range(2):
                    rows = back[b * 512 : (b + 1) * 512, :]
                    out = jnp.dot(rows, secp[ch], preferred_element_type=F32).astype(BF)
                    final_out[b * 512 : (b + 1) * 512, ch * W : (ch + 1) * W] = out
                    yield 0.5

    chains = [[ch * LAG, ch, chain(ch)] for ch in range(CHUNKS)]
    while chains:
        first = min(chains, key=lambda k: (k[0], k[1]))
        pause = next(first[2], None)
        if pause is None:
            chains.remove(first)
        else:
            first[0] += pause

    for b in range(2):
        rows = back[b * 512 : (b + 1) * 512, :]
        near_out[b * 512 : (b + 1) * 512, :] = jnp.dot(rows, nearp[...], preferred_element_type=F32).astype(BF)
    for k in started:
        k.wait_send()


def per_device(residual, code_one, code_two):
    dma = pltpu.SemaphoreType.DMA
    C = CHUNKS
    vmem = pl.BlockSpec(memory_space=pltpu.VMEM)
    return pl.pallas_call(
        main_kernel,
        out_shape=(
            jax.ShapeDtypeStruct((ROWS, D), BF),
            jax.ShapeDtypeStruct((ROWS, D), BF),
        ),
        in_specs=[vmem] * 3,
        out_specs=(vmem, vmem),
        scratch_shapes=[
            pltpu.VMEM((C, GROUPS, CAP, W), BF),
            pltpu.VMEM((C, GROUPS, CAP, W), BF),
            pltpu.VMEM((2, GROUPS, 8, CAP), I32),
            pltpu.VMEM((2, GROUPS, 8, CAP), I32),
            pltpu.VMEM((2, SLOTS, 8), I32),
            pltpu.VMEM((ROWS, 8), I32),
            pltpu.VMEM((2, C, GROUPS, CAP, W), BF),
            pltpu.VMEM((C, GCODES, W), F32),
            pltpu.VMEM((2, C, HALF, W), BF),
            pltpu.VMEM((2, C, HALF, W), BF),
            pltpu.VMEM((2, C, HALF, W), BF),
            pltpu.VMEM((2, C, ZN, ZC, W), BF),
            pltpu.VMEM((2, C, GROUPS, 2, HALF, W), BF),
            pltpu.VMEM((SLOTS, SLOTS), BF),
            pltpu.VMEM((ROWS, SLOTS), BF),
            pltpu.VMEM((C, SLOTS, W), BF),
            pltpu.VMEM((SLOTS, D), F32),
            pltpu.VMEM((SLOTS, D), BF),
            dma((2, GROUPS)), dma((2, GROUPS)),
            dma((2, C, GROUPS)), dma((2, C, GROUPS)),
            dma((2, C)), dma((2, C)),
            dma((2, C, ZN)), dma((2, C, ZN)),
            dma((2, C, ZN)), dma((2, C, ZN)),
            dma((2, C, 20)), dma((2, C, 20)),
            dma((2, C, GROUPS)), dma((2, C, GROUPS)),
        ],
        compiler_params=pltpu.CompilerParams(
            collective_id=0, has_side_effects=True, vmem_limit_bytes=60 * 1024 * 1024
        ),
    )(residual, code_one.reshape(8, CAP), code_two.reshape(8, CAP))


def solution(mesh):
    in_specs = (P(("own", "pair"), None), P(("own", "pair")), P(("own", "pair")))
    out_specs = (P(("own", "pair"), None), P(("own", "pair"), None))
    return jax.shard_map(
        per_device, mesh=mesh, in_specs=in_specs, out_specs=out_specs, check_vma=False
    )
```
